32 devices in a mesh: cfg: 2 (over x), seq: 4 (over z), wblk: 4 (over y, core).
Axes of the slice: x: 2, y: 2, z: 4, core: 2. Of those that a mesh axis runs over, the one named last changes fastest.
Arguments:
- text_tokens: bfloat16 [2, 2, 512, 3072], P('cfg', None, 'seq', 'wblk'), may hold values from -16 to 16
- image_tokens: bfloat16 [2, 4096, 3072], P(None, 'seq', 'wblk'), may hold values from -16 to 16
- pooled_vector: float32 [2, 3072], P('cfg', 'seq'), may hold values from -6 to 6
- mod_weight: bfloat16 [3072, 3, 3072], P('seq', None, 'wblk'), may hold values from -0.109375 to 0.109375
- qkv_weight: bfloat16 [3072, 3, 16, 128], P('seq', None, 'wblk'), may hold values from -0.109375 to 0.109375
- up_weight: bfloat16 [3072, 6144], P('seq', 'wblk'), may hold values from -0.109375 to 0.109375
- query_gain: float32 [128], replicated, may hold values from 0.6 to 10
- key_gain: float32 [128], replicated, may hold values from 0.6 to 10
- attn_weight: bfloat16 [2048, 3072], P('wblk', 'seq'), may hold values from -0.125 to 0.125
- down_weight: bfloat16 [6144, 3072], P('wblk', 'seq'), may hold values from -0.078125 to 0.078125
- lengths: int32 [2], replicated, may hold values from 1 to 512, as said below
- timestep: int32 [1], replicated, may hold values from 0 to 27
Outputs:
- text_out: bfloat16 [2, 2, 512, 3072], P('cfg', None, 'seq', 'wblk')
- velocity: float32 [2, 4096, 3072], P('cfg', 'seq', 'wblk')
- new_image: float32 [2, 4096, 3072], P('cfg', 'seq', 'wblk')
The draws below stay inside these ranges and needn't reach their ends.
Inputs may be any that keep to these rules, and one draw needn't show every extreme that they name: `lengths`: some prompt has all 512 text tokens live in every draw.
All inputs are finite; a program needn't handle non-finite values.
Results may differ from the reference program's by a relative error of at most 0.025.
Values may be sent and summed in bfloat16 or wider, within the bound.
A program may use at most 320 MiB of HBM per device.

```python
import math
import jax
import jax.numpy as jnp
from jax import lax

D = 3072
HEADS = 16
HD = 128
MLP = 6144
TXT = 512
GRID = 64
PROMPTS = 2
STEPS = 28
IMG = 4096
N_WBLK = 4


def gain_drawn(key):
    return jax.random.uniform(jax.random.fold_in(key, 14), (HD,), jnp.float32, 0.6, 1.8)


def draw_query_gain(key, part):
    return gain_drawn(jax.random.fold_in(key, 1))


def draw_key_gain(key, part):
    return gain_drawn(jax.random.fold_in(key, 2))


def draw_lengths(key, part):
    drawn_lengths = jax.random.randint(jax.random.fold_in(key, 3), (PROMPTS,), 1, TXT + 1)
    longest = jax.random.randint(jax.random.fold_in(key, 4), (), 0, PROMPTS)
    return jnp.where(jnp.arange(PROMPTS, dtype=jnp.int32) == longest, TXT, drawn_lengths).astype(jnp.int32)


def feature_tokens(key, shape):
    position = jnp.arange(D, dtype=jnp.float32) / (D - 1)
    ramp = jnp.exp(jnp.log(0.5) + (jnp.log(3.0) - jnp.log(0.5)) * position)
    values = jnp.clip(jax.random.normal(key, shape, jnp.float32), -4.0, 4.0)
    return (values * ramp).astype(jnp.bfloat16)


def draw_text_tokens(key, part):
    return feature_tokens(jax.random.fold_in(key, 21), (2, PROMPTS, TXT, D))


def draw_image_tokens(key, part):
    return feature_tokens(jax.random.fold_in(key, 22), (PROMPTS, IMG, D))


def steps_of(key, dims, cuts, smallest, top_value):
    def one(dim, shards_of):
        draws = jax.random.uniform(jax.random.fold_in(jax.random.fold_in(key, 6), dim), (shards_of,), jnp.float32, smallest / len(cuts), top_value / len(cuts))
        return jnp.repeat(jnp.exp(draws), dims[dim] // shards_of).reshape((-1,) + (1,) * (len(dims) - dim - 1))

    factor_of = one(*cuts[0])
    for cut in cuts[1:]:
        factor_of = factor_of * one(*cut)
    return factor_of


def centred(own_key, dims, deviation, bound, pieces=(), kind=jnp.bfloat16):
    result = jax.random.normal(own_key, dims, jnp.float32) * deviation
    if len(pieces) > 0:
        result = steps_of(own_key, dims, pieces, -0.22, 0.18) * result
    return jnp.clip(result, min=-bound, max=bound).astype(kind)


def setup_inputs(seed: int = 0) -> dict:
    arg_keys = jax.random.split(jax.random.key(seed), 13)
    text_tokens = draw_text_tokens(jax.random.fold_in(arg_keys[12], 71), 0)
    image_tokens = draw_image_tokens(jax.random.fold_in(arg_keys[12], 71), 0)
    pooled_vector = centred(arg_keys[2], (2, D), 1.0, 6.0, ((0, 2), (1, 4)), jnp.float32)
    mod_weight = centred(arg_keys[3], (D, 3, D), D ** -0.5, 0.109375, ((0, 4), (2, 4)))
    qkv_weight = centred(arg_keys[4], (D, 3, HEADS, HD), D ** -0.5, 0.109375, ((0, 4), (2, 4)))
    up_weight = centred(arg_keys[5], (D, MLP), D ** -0.5, 0.109375, ((0, 4), (1, 4)))
    query_gain = draw_query_gain(jax.random.fold_in(arg_keys[12], 71), 0)
    key_gain = draw_key_gain(jax.random.fold_in(arg_keys[12], 71), 0)
    attn_weight = centred(arg_keys[8], (HEADS * HD, D), (HEADS * HD) ** -0.5, 0.125, ((0, 4), (1, 4)))
    down_weight = centred(arg_keys[9], (MLP, D), MLP ** -0.5, 0.078125, ((0, 4), (1, 4)))
    lengths = draw_lengths(jax.random.fold_in(arg_keys[12], 71), 0)
    timestep = jax.random.randint(arg_keys[11], (1,), 0, STEPS).astype(jnp.int32)
    return dict(text_tokens=text_tokens, image_tokens=image_tokens, pooled_vector=pooled_vector, mod_weight=mod_weight, qkv_weight=qkv_weight, up_weight=up_weight, query_gain=query_gain, key_gain=key_gain, attn_weight=attn_weight, down_weight=down_weight, lengths=lengths, timestep=timestep)


epsilon = 1e-06
guidance = 3.5
time_shift = 3.0
rope_theta = 10000.0

def plan(timestep):
    step_index = timestep[0].astype(jnp.float32)
    time_now = 1.0 - step_index / STEPS
    time_next = 1.0 - (step_index + 1.0) / STEPS
    sigma_now = time_shift * time_now / (1.0 + (time_shift - 1.0) * time_now)
    sigma_next = time_shift * time_next / (1.0 + (time_shift - 1.0) * time_next)
    return (sigma_now, sigma_next - sigma_now)

def time_embedding(sigma_now, dim_count):
    halfwidth = dim_count // 2
    frequency = jnp.exp(-math.log(10000.0) * jnp.arange(halfwidth, dtype=jnp.float32) / halfwidth)
    angles = 1000.0 * sigma_now * frequency
    return jnp.concatenate([jnp.cos(angles), jnp.sin(angles)])

def inverse_freq(dim_count):
    return rope_theta ** (-jnp.arange(0, dim_count, 2, dtype=jnp.float32) / dim_count)

def rotary_angles(height_pos, width_pos):
    still_dims = HD // 8
    axis_dims = (HD - still_dims) // 2
    return jnp.concatenate([jnp.zeros((height_pos.shape[0], still_dims // 2), jnp.float32), height_pos[:, None] * inverse_freq(axis_dims)[None], width_pos[:, None] * inverse_freq(axis_dims)[None]], axis=1)

def rotate(vectors, angles):
    paired_dims = vectors.reshape(vectors.shape[:-1] + (HD // 2, 2))
    cosine_table = jnp.cos(angles)[:, None, :]
    sine_table = jnp.sin(angles)[:, None, :]
    first_part = paired_dims[..., 0]
    second_part = paired_dims[..., 1]
    turned = jnp.stack([first_part * cosine_table - second_part * sine_table, first_part * sine_table + second_part * cosine_table], axis=-1)
    return turned.reshape(vectors.shape)

def head_norm(vectors, gain_vector):
    return vectors * lax.rsqrt(lax.optimization_barrier(jnp.mean(vectors * vectors, axis=-1, keepdims=True)) + epsilon) * gain_vector

def layer(tokens, modulation, qkv_weight, up_weight, query_gain, key_gain, attn_weight, down_weight, length, angles):
    seq_len = TXT + IMG
    hidden = tokens.astype(jnp.float32)
    average = lax.optimization_barrier(jnp.mean(hidden, axis=-1, keepdims=True))
    variance = lax.optimization_barrier(jnp.mean(hidden * hidden, axis=-1, keepdims=True)) - average * average
    normed = ((hidden - average) * lax.rsqrt(variance + epsilon) * (1.0 + modulation[1]) + modulation[0]).astype(jnp.bfloat16)
    projected = jnp.dot(normed, qkv_weight.reshape(D, 3 * HEADS * HD), preferred_element_type=jnp.float32)
    projected = projected.reshape(seq_len, 3, HEADS, HD)
    mlp_units = jnp.dot(normed, up_weight, preferred_element_type=jnp.float32)
    queries = rotate(head_norm(projected[:, 0], query_gain), angles).astype(jnp.bfloat16)
    key_rows = rotate(head_norm(projected[:, 1], key_gain), angles).astype(jnp.bfloat16)
    values = projected[:, 2].astype(jnp.bfloat16)
    positions = jnp.arange(seq_len, dtype=jnp.int32)
    key_live = (positions >= TXT) | (positions < length)

    def one_head(head_index):
        query_head = lax.dynamic_index_in_dim(queries, head_index, 1, keepdims=False)
        key_head = lax.dynamic_index_in_dim(key_rows, head_index, 1, keepdims=False)
        value_head = lax.dynamic_index_in_dim(values, head_index, 1, keepdims=False)
        scores = jnp.dot(query_head, key_head.T, preferred_element_type=jnp.float32) * HD ** (-0.5)
        scores = jnp.where(key_live[None, :], scores, -1e+30)
        top_score = lax.optimization_barrier(jnp.max(scores, axis=-1, keepdims=True))
        weights = jnp.exp(scores - top_score)
        denominator = lax.optimization_barrier(jnp.sum(weights, axis=-1, keepdims=True))
        mixed = jnp.dot(weights.astype(jnp.bfloat16), value_head, preferred_element_type=jnp.float32)
        return (mixed / denominator).astype(jnp.bfloat16)
    attended = lax.map(one_head, jnp.arange(HEADS, dtype=jnp.int32))
    attended = attended.transpose(1, 0, 2).reshape(seq_len, HEADS * HD)
    activated = jax.nn.gelu(mlp_units, approximate=True).astype(jnp.bfloat16)
    head_block = HEADS // N_WBLK * HD
    unit_block = MLP // N_WBLK
    branch = jnp.zeros((seq_len, D), jnp.float32)
    for block_index in range(N_WBLK):
        block_term = jnp.dot(attended[:, block_index * head_block:(block_index + 1) * head_block], attn_weight[block_index * head_block:(block_index + 1) * head_block], preferred_element_type=jnp.float32)
        block_term = block_term + jnp.dot(activated[:, block_index * unit_block:(block_index + 1) * unit_block], down_weight[block_index * unit_block:(block_index + 1) * unit_block], preferred_element_type=jnp.float32)
        rounded = lax.optimization_barrier(block_term.astype(jnp.bfloat16))
        branch = branch + rounded.astype(jnp.float32)
    return hidden + modulation[2] * branch

def reference(text_tokens, image_tokens, pooled_vector, mod_weight, qkv_weight, up_weight, query_gain, key_gain, attn_weight, down_weight, lengths, timestep):
    sigma_now, step_size = plan(timestep)
    cond_vec = jax.nn.silu(pooled_vector + time_embedding(sigma_now, D)[None]).astype(jnp.bfloat16)
    modulation = jnp.dot(cond_vec, mod_weight.reshape(D, 3 * D), preferred_element_type=jnp.float32).reshape(2, 3, D)
    image_index = jnp.arange(IMG, dtype=jnp.int32)
    height_pos = jnp.concatenate([jnp.zeros((TXT,), jnp.float32), (image_index // GRID).astype(jnp.float32)])
    width_pos = jnp.concatenate([jnp.zeros((TXT,), jnp.float32), (image_index % GRID).astype(jnp.float32)])
    angles = rotary_angles(height_pos, width_pos)
    text_halves = []
    image_halves = []
    for half_index in range(2):
        text_list = []
        image_list = []
        for prompt in range(PROMPTS):
            tokens = jnp.concatenate([text_tokens[half_index, prompt], image_tokens[prompt]], axis=0)
            layer_out = layer(tokens, modulation[half_index], qkv_weight, up_weight, query_gain, key_gain, attn_weight, down_weight, lengths[prompt], angles)
            text_list.append(layer_out[:TXT].astype(jnp.bfloat16))
            image_list.append(layer_out[TXT:])
        text_halves.append(jnp.stack(text_list))
        image_halves.append(jnp.stack(image_list))
    text_out = jnp.stack(text_halves)
    velocity = image_halves[1] + guidance * (image_halves[0] - image_halves[1])
    new_image = image_tokens.astype(jnp.float32) + step_size * velocity
    return (text_out, velocity, new_image)
```

```python
import functools
import math

import jax
import jax.numpy as jnp
from jax import lax
from jax.experimental import pallas as pl
from jax.experimental.pallas import tpu as pltpu
from jax.sharding import PartitionSpec as P

D = 3072
HD = 128
GRID = 64
STEPS = 28

epsilon = 1e-06
guidance = 3.5
time_shift = 3.0
rope_theta = 10000.0
VMEM = 60 * 1024 * 1024


def plan(timestep):
    step_index = timestep[0].astype(jnp.float32)
    time_now = 1.0 - step_index / STEPS
    time_next = 1.0 - (step_index + 1.0) / STEPS
    sigma_now = time_shift * time_now / (1.0 + (time_shift - 1.0) * time_now)
    sigma_next = time_shift * time_next / (1.0 + (time_shift - 1.0) * time_next)
    return (sigma_now, sigma_next - sigma_now)


def time_embedding(sigma_now, dim_count):
    halfwidth = dim_count // 2
    frequency = jnp.exp(-math.log(10000.0) * jnp.arange(halfwidth, dtype=jnp.float32) / halfwidth)
    angles = 1000.0 * sigma_now * frequency
    return jnp.concatenate([jnp.cos(angles), jnp.sin(angles)])


def inverse_freq(dim_count):
    return rope_theta ** (-jnp.arange(0, dim_count, 2, dtype=jnp.float32) / dim_count)


def rotary_angles(height_pos, width_pos):
    still_dims = HD // 8
    axis_dims = (HD - still_dims) // 2
    return jnp.concatenate(
        [
            jnp.zeros((height_pos.shape[0], still_dims // 2), jnp.float32),
            height_pos[:, None] * inverse_freq(axis_dims)[None],
            width_pos[:, None] * inverse_freq(axis_dims)[None],
        ],
        axis=1,
    )


def largest_block(rows, limit, unit=16):
    best = rows
    for size in range(unit, min(rows, limit) + 1, unit):
        if rows % size == 0:
            best = size
    return best


def qkv_body(heads, x_ref, w_ref, cos_ref, sin_ref, gain_ref, out_ref):
    result = jnp.dot(x_ref[0, 0], w_ref[...], preferred_element_type=jnp.float32)
    cosine = cos_ref[...]
    sine = sin_ref[...]
    even = lax.broadcasted_iota(jnp.int32, cosine.shape, 1) % 2 == 0
    for head in range(heads):
        for kind in range(3):
            start = (kind * heads + head) * HD
            part = result[:, start : start + HD]
            if kind < 2:
                mean_sq = jnp.mean(part * part, axis=-1, keepdims=True)
                part = part * lax.rsqrt(mean_sq + epsilon) * gain_ref[kind : kind + 1]
                other = jnp.where(even, pltpu.roll(part, HD - 1, 1), pltpu.roll(part, 1, 1))
                part = part * cosine + other * sine
            out_ref[0, 0, head, kind] = part.astype(jnp.bfloat16)


def project_qkv(normed, weight, cosine, sine, gains, heads):
    halves, prompts, rows, _ = normed.shape
    block = largest_block(rows, 384)
    grid = (halves, prompts, rows // block)
    return pl.pallas_call(
        functools.partial(qkv_body, heads),
        grid=grid,
        in_specs=[
            pl.BlockSpec((1, 1, block, D), lambda c, p, i: (c, p, i, 0)),
            pl.BlockSpec((D, 3 * heads * HD), lambda c, p, i: (0, 0)),
            pl.BlockSpec((block, HD), lambda c, p, i: (i, 0)),
            pl.BlockSpec((block, HD), lambda c, p, i: (i, 0)),
            pl.BlockSpec((2, HD), lambda c, p, i: (0, 0)),
        ],
        out_specs=pl.BlockSpec((1, 1, heads, 3, block, HD), lambda c, p, i: (c, p, 0, 0, i, 0)),
        out_shape=jax.ShapeDtypeStruct((halves, prompts, heads, 3, rows, HD), jnp.bfloat16),
        compiler_params=pltpu.CompilerParams(vmem_limit_bytes=VMEM),
        cost_estimate=pl.CostEstimate(
            flops=2 * halves * prompts * rows * D * 3 * heads * HD,
            bytes_accessed=2 * halves * prompts * rows * D + 6 * D * heads * HD,
            transcendentals=0,
        ),
        name="project_qkv",
    )(normed, weight, cosine, sine, gains)


def attention_body(shards_of, rows, text_rows, live_ref, q_ref, k_ref, v_ref, out_ref):
    unit = pl.program_id(0)
    live = live_ref[unit]
    factor = HD ** (-0.5) * math.log2(math.e)
    queries = q_ref[0, 0, 0]
    image_rows = rows - text_rows
    first = image_rows // HD * HD

    def score(shard):
        part = lax.dot_general(
            queries, k_ref[shard, 0, 0], (((1,), (1,)), ((), ())), preferred_element_type=jnp.float32
        )
        tail = part[:, first:]
        column = lax.broadcasted_iota(jnp.int32, tail.shape, 1) + (first - image_rows)
        tail = jnp.where((column < 0) | (column + shard * text_rows < live), tail, -1e30)
        if first == 0:
            return tail
        return jnp.concatenate([part[:, :first], tail], axis=1)

    top = None
    following = score(0)
    for shard in range(shards_of):
        scores = following
        if shard + 1 < shards_of:
            following = score(shard + 1)
        highest = jnp.max(scores, axis=-1, keepdims=True)
        if top is not None:
            highest = jnp.maximum(top, highest)
        weights = jnp.exp2((scores - highest) * factor)
        total = jnp.sum(weights, axis=-1, keepdims=True)
        mixed = jnp.dot(
            weights.astype(jnp.bfloat16), v_ref[shard, 0, 0], preferred_element_type=jnp.float32
        )
        if top is not None:
            shrink = jnp.exp2((top - highest) * factor)
            total = total + denominator * shrink
            mixed = mixed + numerator * shrink
        top, denominator, numerator = highest, total, mixed
    out_ref[0, 0] = (numerator / denominator).astype(jnp.bfloat16)


def attention(live, queries, keys_values, text_rows):
    query_shards, units, _, rows, _ = queries.shape
    shards_of = keys_values.shape[0]
    block = largest_block(rows, 384)
    return pl.pallas_call(
        functools.partial(attention_body, shards_of, rows, text_rows),
        grid_spec=pltpu.PrefetchScalarGridSpec(
            num_scalar_prefetch=1,
            grid=(units, query_shards, rows // block),
            in_specs=[
                pl.BlockSpec((1, 1, 1, block, HD), lambda u, s, i, live: (s, u, 0, i, 0)),
                pl.BlockSpec((shards_of, 1, 1, rows, HD), lambda u, s, i, live: (0, u, 1, 0, 0)),
                pl.BlockSpec((shards_of, 1, 1, rows, HD), lambda u, s, i, live: (0, u, 2, 0, 0)),
            ],
            out_specs=pl.BlockSpec((1, 1, block, HD), lambda u, s, i, live: (s, u, i, 0)),
        ),
        out_shape=jax.ShapeDtypeStruct((query_shards, units, rows, HD), jnp.bfloat16),
        compiler_params=pltpu.CompilerParams(vmem_limit_bytes=VMEM),
        cost_estimate=pl.CostEstimate(
            flops=4 * query_shards * units * rows * shards_of * rows * HD,
            bytes_accessed=8 * query_shards * units * rows * HD,
            transcendentals=query_shards * units * rows * shards_of * rows,
        ),
        name="attention",
    )(live, queries, keys_values, keys_values)


def guided_body(heads, col_blocks, att_ref, act_ref, w_ref, gate_ref, out_ref):
    width = w_ref.shape[2]
    block = out_ref.shape[1]
    stacked = []
    for half in range(2):
        pieces = [att_ref[half, 0, head] for head in range(heads)] + [act_ref[half, 0]]
        stacked.append(jnp.concatenate(pieces, axis=1))
    terms = jnp.concatenate(stacked, axis=0)
    for col in range(col_blocks):
        part = jnp.dot(terms, w_ref[col], preferred_element_type=jnp.float32)
        span = slice(col * width, (col + 1) * width)
        guided = part[:block] * (guidance * gate_ref[0:1, span])
        guided = guided - part[block:] * ((guidance - 1.0) * gate_ref[1:2, span])
        out_ref[0, :, span] = guided.astype(jnp.bfloat16)


def guided_terms(attended, activated, weight, gate, image_rows):
    halves, prompts, heads, rows, _ = attended.shape
    units = activated.shape[3]
    col_blocks, depth, width = weight.shape
    block = largest_block(image_rows, 256)
    return pl.pallas_call(
        functools.partial(guided_body, heads, col_blocks),
        grid=(prompts, image_rows // block),
        in_specs=[
            pl.BlockSpec((2, 1, heads, block, HD), lambda p, i: (0, p, 0, i, 0)),
            pl.BlockSpec((2, 1, block, units), lambda p, i: (0, p, i, 0)),
            pl.BlockSpec((col_blocks, depth, width), lambda p, i: (0, 0, 0)),
            pl.BlockSpec((2, D), lambda p, i: (0, 0)),
        ],
        out_specs=pl.BlockSpec((1, block, D), lambda p, i: (p, i, 0)),
        out_shape=jax.ShapeDtypeStruct((prompts, image_rows, D), jnp.bfloat16),
        compiler_params=pltpu.CompilerParams(vmem_limit_bytes=VMEM),
        cost_estimate=pl.CostEstimate(
            flops=4 * prompts * image_rows * depth * D,
            bytes_accessed=2 * (prompts * image_rows * (2 * depth + D) + depth * D),
            transcendentals=0,
        ),
        name="guided_terms",
    )(attended, activated, weight, gate)


CORE_SWAP = [(0, 1), (1, 0), (2, 3), (3, 2)]
CHIP_SWAP = [(0, 2), (2, 0), (1, 3), (3, 1)]


def gather_features(block, wblk_pos, wblk_size):
    if wblk_size != 4:
        return lax.all_gather(block, "wblk", axis=block.ndim - 1, tiled=True)
    far = lax.ppermute(block, "wblk", CHIP_SWAP)
    near = lax.ppermute(block, "wblk", CORE_SWAP)
    far_near = lax.ppermute(far, "wblk", CORE_SWAP)
    odd = wblk_pos % 2 == 1
    here = jnp.where(odd, jnp.concatenate([near, block], -1), jnp.concatenate([block, near], -1))
    there = jnp.where(odd, jnp.concatenate([far_near, far], -1), jnp.concatenate([far, far_near], -1))
    upper = wblk_pos >= 2
    return jnp.where(upper, jnp.concatenate([there, here], -1), jnp.concatenate([here, there], -1))


def scatter_features(terms, wblk_pos, wblk_size):
    last = terms.ndim - 1
    if wblk_size != 4:
        summed = lax.psum_scatter(terms, "wblk", scatter_dimension=last, tiled=True)
        return summed.astype(jnp.float32)
    width = terms.shape[last] // 4

    def block(array, index):
        return lax.dynamic_slice_in_dim(array, index * width, width, last)

    core_mate = wblk_pos + 1 - 2 * (wblk_pos % 2)
    chip_mate = (wblk_pos + 2) % 4
    both_mate = (core_mate + 2) % 4
    far_part = block(terms, chip_mate).astype(jnp.float32) + lax.ppermute(
        block(terms, both_mate), "wblk", CORE_SWAP
    ).astype(jnp.float32)
    far_sum = lax.ppermute(far_part.astype(jnp.bfloat16), "wblk", CHIP_SWAP).astype(jnp.float32)
    near_part = lax.ppermute(block(terms, core_mate), "wblk", CORE_SWAP).astype(jnp.float32)
    return block(terms, wblk_pos).astype(jnp.float32) + near_part + far_sum


def shards(
    cfg_size,
    seq_size,
    wblk_size,
    text_tokens,
    image_tokens,
    pooled_vector,
    mod_weight,
    qkv_weight,
    up_weight,
    query_gain,
    key_gain,
    attn_weight,
    down_weight,
    lengths,
    timestep,
):
    seq_pos = lax.axis_index("seq")
    cfg_pos = lax.axis_index("cfg")
    wblk_pos = lax.axis_index("wblk")
    prompts, image_rows, dim_local = image_tokens.shape
    text_rows = text_tokens.shape[2]
    local_len = text_rows + image_rows
    dim_seq = pooled_vector.shape[1]
    heads = qkv_weight.shape[2] // cfg_size
    units = up_weight.shape[1] // cfg_size

    qkv_part = lax.dynamic_slice_in_dim(qkv_weight, cfg_pos * heads, heads, 2)
    qkv_part = qkv_part.reshape(dim_seq, 3 * heads * HD)
    qkv_full = lax.all_gather(qkv_part, "seq", axis=0, tiled=True)
    up_part = lax.dynamic_slice_in_dim(up_weight, cfg_pos * units, units, 1)
    up_full = lax.all_gather(up_part, "seq", axis=0, tiled=True)
    out_part = jnp.concatenate(
        [
            lax.dynamic_slice_in_dim(attn_weight, cfg_pos * heads * HD, heads * HD, 0),
            lax.dynamic_slice_in_dim(down_weight, cfg_pos * units, units, 0),
        ],
        axis=0,
    )
    out_full = lax.all_gather(out_part, "seq", axis=0)

    text_other = lax.ppermute(text_tokens[0], "cfg", [(0, 1), (1, 0)])
    text_both = jnp.where(
        cfg_pos == 0, jnp.stack([text_tokens[0], text_other]), jnp.stack([text_other, text_tokens[0]])
    )
    image_full = gather_features(image_tokens, wblk_pos, wblk_size)
    text_full = gather_features(text_both, wblk_pos, wblk_size)

    sigma_now, step_size = plan(timestep)
    embedded = lax.dynamic_slice_in_dim(time_embedding(sigma_now, D), seq_pos * dim_seq, dim_seq)
    cond_vec = jax.nn.silu(pooled_vector[0] + embedded).astype(jnp.bfloat16)[None]
    mod_terms = jnp.dot(
        cond_vec, mod_weight.reshape(dim_seq, 3 * dim_local), preferred_element_type=jnp.float32
    )
    placed = lax.dynamic_update_slice(
        jnp.zeros((2, 3, D), jnp.float32),
        mod_terms.reshape(1, 3, dim_local),
        (cfg_pos, 0, wblk_pos * dim_local),
    )
    modulation = lax.psum(placed, ("cfg", "seq", "wblk"))

    def standard(rows):
        hidden = rows.astype(jnp.float32)
        average = jnp.mean(hidden, axis=-1, keepdims=True)
        variance = jnp.mean(hidden * hidden, axis=-1, keepdims=True) - average * average
        return average, lax.rsqrt(variance + epsilon)

    image_mean, image_rstd = standard(image_full)
    text_mean, text_rstd = standard(text_full)
    rows_both = jnp.concatenate(
        [jnp.broadcast_to(image_full[None], (2,) + image_full.shape), text_full], axis=2
    )
    mean_both = jnp.concatenate(
        [jnp.broadcast_to(image_mean[None], (2,) + image_mean.shape), text_mean], axis=2
    )
    rstd_both = jnp.concatenate(
        [jnp.broadcast_to(image_rstd[None], (2,) + image_rstd.shape), text_rstd], axis=2
    )
    normed = (
        (rows_both.astype(jnp.float32) - mean_both)
        * rstd_both
        * (1.0 + modulation[:, 1])[:, None, None]
        + modulation[:, 0][:, None, None]
    ).astype(jnp.bfloat16)

    image_index = seq_pos * image_rows + jnp.arange(image_rows, dtype=jnp.int32)
    zeros = jnp.zeros((text_rows,), jnp.float32)
    height_pos = jnp.concatenate([(image_index // GRID).astype(jnp.float32), zeros])
    width_pos = jnp.concatenate([(image_index % GRID).astype(jnp.float32), zeros])
    angles = jnp.repeat(rotary_angles(height_pos, width_pos), 2, axis=1)
    signs = jnp.where(jnp.arange(HD) % 2 == 0, -1.0, 1.0).astype(jnp.float32)
    gains = jnp.stack([query_gain, key_gain])
    qkv = project_qkv(normed, qkv_full, jnp.cos(angles), jnp.sin(angles) * signs, gains, heads)

    count = 2 * prompts * heads
    qkv = qkv.reshape(count, 3, local_len, HD)
    if count % seq_size == 0:
        own = count // seq_size
        mixed = lax.all_to_all(
            qkv.reshape(seq_size, own, 3, local_len, HD), "seq", split_axis=0, concat_axis=0, tiled=True
        )
        unit_index = seq_pos * own + jnp.arange(own, dtype=jnp.int32)
        live = lengths[(unit_index // heads) % prompts]
        attended = attention(live, mixed, mixed, text_rows)
        attended = lax.all_to_all(attended, "seq", split_axis=0, concat_axis=0, tiled=True)
    else:
        keys_values = lax.all_gather(qkv, "seq", axis=0)
        live = lengths[(jnp.arange(count, dtype=jnp.int32) // heads) % prompts]
        attended = attention(live, qkv[None], keys_values, text_rows)
    attended = attended.reshape(2, prompts, heads, local_len, HD)

    mlp_units = jnp.dot(
        normed.reshape(2 * prompts * local_len, D), up_full, preferred_element_type=jnp.float32
    )
    activated = jax.nn.gelu(mlp_units, approximate=True).astype(jnp.bfloat16)
    activated = activated.reshape(2, prompts, local_len, units)

    guided = guided_terms(attended, activated, out_full, modulation[:, 2], image_rows)
    text_att = attended[:, :, :, image_rows:].transpose(0, 1, 3, 2, 4)
    text_att = text_att.reshape(2, prompts, text_rows, heads * HD)
    text_in = jnp.concatenate([text_att, activated[:, :, image_rows:]], axis=-1)
    text_terms = jnp.einsum("cprk,skd->cprsd", text_in, out_full, preferred_element_type=jnp.float32)
    text_terms = text_terms.reshape(2, prompts, text_rows, D).astype(jnp.bfloat16)

    own_prompts = prompts // 2
    image_sum = scatter_features(guided, wblk_pos, wblk_size)
    image_sum = image_sum.reshape((2, own_prompts) + image_sum.shape[1:])
    text_sum = scatter_features(text_terms, wblk_pos, wblk_size)

    def swap_halves(pairs):
        kept = lax.dynamic_index_in_dim(pairs, cfg_pos, 0, keepdims=False)
        given = lax.dynamic_index_in_dim(pairs, 1 - cfg_pos, 0, keepdims=False)
        taken = lax.ppermute(given.astype(jnp.bfloat16), "cfg", [(0, 1), (1, 0)])
        return kept + taken.astype(jnp.float32)

    text_branch = swap_halves(text_sum)
    image_branch = swap_halves(image_sum)
    own_gate = lax.dynamic_slice(modulation, (cfg_pos, 2, wblk_pos * dim_local), (1, 1, dim_local))
    text_out = (text_tokens[0].astype(jnp.float32) + own_gate * text_branch).astype(jnp.bfloat16)[None]
    latent = lax.dynamic_slice_in_dim(image_tokens, cfg_pos * own_prompts, own_prompts, 0).astype(
        jnp.float32
    )
    velocity = latent + image_branch
    new_image = latent + step_size * velocity
    return (text_out, velocity, new_image)


def solution(mesh):
    in_specs = (
        P("cfg", None, "seq", "wblk"),
        P(None, "seq", "wblk"),
        P("cfg", "seq"),
        P("seq", None, "wblk"),
        P("seq", None, "wblk", None),
        P("seq", "wblk"),
        P(),
        P(),
        P("wblk", "seq"),
        P("wblk", "seq"),
        P(),
        P(),
    )
    out_specs = (P("cfg", None, "seq", "wblk"), P("cfg", "seq", "wblk"), P("cfg", "seq", "wblk"))
    sizes = (mesh.shape["cfg"], mesh.shape["seq"], mesh.shape["wblk"])
    return jax.shard_map(
        functools.partial(shards, *sizes),
        mesh=mesh,
        in_specs=in_specs,
        out_specs=out_specs,
        check_vma=False,
    )
```
